32 devices in a mesh: dp: 16 (over z, y, core), fsdp: 2 (over x).
Axes of the slice: x: 2, y: 2, z: 4, core: 2. Of those that a mesh axis runs over, the one named last changes fastest.
Arguments:
- hidden: bfloat16 [16384, 1152], P(('dp', 'fsdp')), may hold values from -6 to 6
- text_ids: int32 [1024, 16], P(('dp', 'fsdp')), may hold values from 0 to 31999, as said below
- ln_gain: float32 [1152], replicated, may hold values from 0.5 to 1.5
- ln_bias: float32 [1152], replicated, may hold values from -2 to 2
- fc1_weight: bfloat16 [1152, 4304], P(None, 'fsdp'), may hold values from -0.1875 to 0.1875
- fc1_bias: float32 [4304], replicated, may hold values from -3 to 3
- fc2_weight: bfloat16 [4304, 1152], P('fsdp'), may hold values from -0.09375 to 0.09375
- fc2_bias: float32 [1152], replicated, may hold values from -3 to 3
- final_gain: float32 [1152], replicated, may hold values from 0.5 to 1.5
- final_bias: float32 [1152], replicated, may hold values from -0.2 to 0.2
- head_weight: bfloat16 [1152, 1152], replicated, may hold values from -0.1875 to 0.1875
- head_bias: float32 [1152], replicated, may hold values from -0.3 to 0.3
- image_emb: bfloat16 [1024, 1152], P(('dp', 'fsdp')), may hold values from -6 to 6
- teacher_logits: bfloat16 [1024, 12, 64], P('dp', None, 'fsdp'), may hold values from -12 to 12
- logit_scale: float32 [1], replicated, may hold values from 4 to 16
- logit_bias: float32 [1], replicated, may hold values from -3 to 0
Outputs:
- image_grad: float32 [1024, 1152], P(('dp', 'fsdp'))
The draws below stay inside these ranges and needn't reach their ends.
Inputs may be any that keep to these rules, and one draw needn't show every extreme that they name: `text_ids`: 0 marks padding after a text's end; every text has at least one token and the tokens of a text come first.
All inputs are finite; a program needn't handle non-finite values.
Results may differ from the reference program's by a relative error of at most 0.0018.
Values may be sent and summed in bfloat16 or wider, within the bound.
A program may use at most 128 MiB of HBM per device.

```python
import math
import jax
import jax.numpy as jnp
from jax import lax

D = 1152
FF = 4304
VOCAB = 32000
SEQ = 16
WINDOW = 12
PAIRS_DEV = 32
GROUP = 64
TEXTS = 1024
TOKENS = 16384
N_DP = 16


def draw_text_ids(key, part):
    key_len, key_ids = jax.random.split(jax.random.fold_in(key, 7))
    lengths = jax.random.randint(key_len, (TEXTS, 1), 1, SEQ + 1)
    lengths = lengths.at[0, 0].set(1)
    tokens = jax.random.randint(key_ids, (TEXTS, SEQ), 1, VOCAB)
    tokens = tokens.at[0, 0].set(VOCAB - 1)
    place = jnp.arange(SEQ)[None, :]
    return jnp.where(place < lengths, tokens, 0).astype(jnp.int32)


def steps_of(stream_key, shape, cuts, low, largest):
    loudness = 1.0
    for dim, parts in cuts:
        steps = jax.random.uniform(jax.random.fold_in(jax.random.fold_in(stream_key, 6), dim), (parts,), jnp.float32, low / len(cuts), largest / len(cuts))
        loudness = loudness * jnp.repeat(jnp.exp(steps), shape[dim] // parts).reshape((-1,) + (1,) * (len(shape) - 1 - dim))
    return loudness


def normal_values(rng, shape, scale, reach, cuts=(), kind=jnp.bfloat16):
    drawn = scale * jax.random.normal(rng, shape, jnp.float32)
    if cuts:
        drawn = drawn * steps_of(rng, shape, cuts, -0.22, 0.18)
    return jnp.clip(drawn, -reach, reach).astype(kind)


def setup_inputs(seed: int = 0) -> dict:
    arg_keys = jax.random.split(jax.random.key(seed), 17)
    return {
        "hidden": normal_values(arg_keys[0], (TOKENS, D), 1.0, 6.0, ((0, 32),)),
        "text_ids": draw_text_ids(jax.random.fold_in(arg_keys[16], 71), 0),
        "ln_gain": jnp.clip(1.0 + 0.1 * jax.random.normal(arg_keys[2], (D,), jnp.float32), 0.5, 1.5),
        "ln_bias": normal_values(arg_keys[3], (D,), 0.3, 2.0, (), jnp.float32),
        "fc1_weight": normal_values(arg_keys[4], (D, FF), D ** -0.5, 0.1875, ((1, 2),)),
        "fc1_bias": normal_values(arg_keys[5], (FF,), 0.5, 3.0, (), jnp.float32),
        "fc2_weight": normal_values(arg_keys[6], (FF, D), FF ** -0.5, 0.09375, ((0, 2),)),
        "fc2_bias": normal_values(arg_keys[7], (D,), 0.5, 3.0, (), jnp.float32),
        "final_gain": jnp.clip(1.0 + 0.1 * jax.random.normal(arg_keys[8], (D,), jnp.float32), 0.5, 1.5),
        "final_bias": normal_values(arg_keys[9], (D,), 0.03, 0.2, (), jnp.float32),
        "head_weight": normal_values(arg_keys[10], (D, D), D ** -0.5, 0.1875),
        "head_bias": normal_values(arg_keys[11], (D,), 0.05, 0.3, (), jnp.float32),
        "image_emb": normal_values(arg_keys[12], (TEXTS, D), 1.0, 6.0, ((0, 32),)),
        "teacher_logits": normal_values(arg_keys[13], (TEXTS, WINDOW, GROUP), 3.0, 12.0, ((0, 16), (2, 2))),
        "logit_scale": jnp.clip(jnp.exp(jax.random.uniform(arg_keys[14], (1,), jnp.float32, math.log(4.0), math.log(16.0))), 4.0, 16.0),
        "logit_bias": jnp.clip(jax.random.uniform(arg_keys[15], (1,), jnp.float32, -3.0, 0.0), -3.0, 0.0),
    }


def layer_norm(values, gain, shift):
    centre = lax.optimization_barrier(jnp.mean(values, axis=-1, keepdims=True))
    spread = lax.optimization_barrier(jnp.mean((values - centre) ** 2, axis=-1, keepdims=True))
    return (values - centre) * lax.rsqrt(spread + 1e-06) * gain + shift

def reference(hidden, text_ids, ln_gain, ln_bias, fc1_weight, fc1_bias, fc2_weight, fc2_bias, final_gain, final_bias, head_weight, head_bias, image_emb, teacher_logits, logit_scale, logit_bias):
    blocks = hidden.reshape(-1, PAIRS_DEV * SEQ, D)
    id_blocks = text_ids.reshape(-1, PAIRS_DEV, SEQ)

    def encode(pair):
        tokens, ids = pair
        flat = tokens.astype(jnp.float32)
        normed = layer_norm(flat, ln_gain, ln_bias).astype(jnp.bfloat16)
        pre = jnp.dot(normed, fc1_weight, preferred_element_type=jnp.float32) + fc1_bias
        act = jax.nn.gelu(pre, approximate=True).astype(jnp.bfloat16)
        out = flat + jnp.dot(act, fc2_weight, preferred_element_type=jnp.float32) + fc2_bias
        final = layer_norm(out, final_gain, final_bias).reshape(PAIRS_DEV, SEQ, D)
        keep = (ids != 0).astype(jnp.float32)
        pooled = lax.optimization_barrier(jnp.sum(final * keep[:, :, None], axis=1)) / lax.optimization_barrier(jnp.sum(keep, axis=1))[:, None]
        emb = jnp.dot(pooled.astype(jnp.bfloat16), head_weight, preferred_element_type=jnp.float32) + head_bias
        return (emb * lax.rsqrt(lax.optimization_barrier(jnp.sum(emb * emb, axis=-1, keepdims=True)) + 1e-06)).astype(jnp.bfloat16)
    units = lax.map(encode, (blocks, id_blocks)).reshape(N_DP, -1, D)
    images = image_emb.astype(jnp.float32)
    image_unit = (images * lax.rsqrt(lax.optimization_barrier(jnp.sum(images * images, axis=-1, keepdims=True)) + 1e-06)).astype(jnp.bfloat16)
    image_unit = image_unit.reshape(N_DP, -1, D).astype(jnp.float32)
    teach = teacher_logits.reshape(N_DP, -1, WINDOW, teacher_logits.shape[2])
    scale = logit_scale[0]
    offset = logit_bias[0]
    total = jnp.zeros(image_unit.shape, jnp.float32)
    for step in range(WINDOW):
        texts = jnp.roll(units, step, axis=0).astype(jnp.float32)
        target = jax.nn.sigmoid(jnp.roll(teach[:, :, step, :], step, axis=0).astype(jnp.float32))
        score = scale * jnp.einsum('kgd,kjd->kgj', texts, image_unit) + offset
        weight = (jax.nn.sigmoid(score) - target).astype(jnp.bfloat16).astype(jnp.float32)
        total = total + jnp.einsum('kgj,kgd->kjd', weight, texts)
    return (scale * total).reshape(-1, D)
```

```python
import functools

import jax
import jax.numpy as jnp
from jax import lax
from jax.experimental import pallas as pl
from jax.experimental.pallas import tpu as pltpu
from jax.sharding import PartitionSpec as P

MESH = pl.DeviceIdType.MESH
F32 = jnp.float32
BF16 = jnp.bfloat16


def layer_norm(values, gain, shift):
    centre = jnp.mean(values, axis=-1, keepdims=True)
    moved = values - centre
    spread = jnp.mean(moved * moved, axis=-1, keepdims=True)
    return moved * lax.rsqrt(spread + 1e-06) * gain + shift


def unit_rows(values):
    return values * lax.rsqrt(jnp.sum(values * values, axis=-1, keepdims=True) + 1e-06)


def mlp_kernel(
    n,
    chunk,
    tile,
    seq,
    hidden,
    keep,
    ln_gain,
    ln_bias,
    fc1_hbm,
    fc1_bias,
    fc2_hbm,
    fc2_bias,
    final_gain,
    final_bias,
    head_hbm,
    head_bias,
    unit,
    fc1,
    fc2,
    head,
    normed,
    total,
    theirs,
    back,
    parts,
    pooled,
    load_sem,
    send_sem,
    recv_sem,
    back_send,
    back_recv,
):
    dp = lax.axis_index("dp")
    me = lax.axis_index("fsdp")
    tokens = hidden.shape[0]
    units = fc1.shape[1]
    chunks = tokens // chunk
    loads = [
        pltpu.make_async_copy(src, dst, load_sem.at[i])
        for i, (src, dst) in enumerate(((fc1_hbm, fc1), (fc2_hbm, fc2), (head_hbm, head)))
    ]
    for load in loads:
        load.start()

    def ahead(by):
        return (dp, lax.rem(me + by + n, n))

    barrier = pltpu.get_barrier_semaphore()
    for by in range(1, n):
        pl.semaphore_signal(barrier, inc=1, device_id=ahead(by), device_id_type=MESH)
    pl.semaphore_wait(barrier, n - 1)

    def outward(by, c):
        rows = pl.ds(c * chunk, chunk)
        return pltpu.make_async_remote_copy(
            src_ref=normed.at[rows],
            dst_ref=theirs.at[by - 1, rows],
            send_sem=send_sem.at[by - 1, c],
            recv_sem=recv_sem.at[by - 1, c],
            device_id=ahead(by),
            device_id_type=MESH,
        )

    def homeward(by, c):
        rows = pl.ds(c * chunk, chunk)
        return pltpu.make_async_remote_copy(
            src_ref=back.at[by - 1, rows],
            dst_ref=parts.at[by - 1, rows],
            send_sem=back_send.at[by - 1, c],
            recv_sem=back_recv.at[by - 1, c],
            device_id=ahead(-by),
            device_id_type=MESH,
        )

    def norm_step(c, _):
        rows = pl.ds(pl.multiple_of(c * chunk, chunk), chunk)
        normed[rows, :] = layer_norm(
            hidden[rows, :].astype(F32), ln_gain[...], ln_bias[...]
        ).astype(BF16)
        for by in range(1, n):
            outward(by, c).start()
        return 0

    lax.fori_loop(0, chunks, norm_step, 0)
    loads[0].wait()
    loads[1].wait()

    def mlp(values):
        mixed = None
        for low in range(0, units, tile):
            high = min(low + tile, units)
            pre = jnp.dot(values, fc1[:, low:high], preferred_element_type=F32)
            act = jax.nn.gelu(pre + fc1_bias[:, low:high], approximate=True).astype(BF16)
            term = jnp.dot(act, fc2[low:high, :], preferred_element_type=F32)
            mixed = term if mixed is None else mixed + term
        return mixed

    def own_step(c, _):
        rows = pl.ds(pl.multiple_of(c * chunk, chunk), chunk)
        total[rows, :] = mlp(normed[rows, :]) + hidden[rows, :].astype(F32) + fc2_bias[...]
        return 0

    lax.fori_loop(0, chunks, own_step, 0)

    for by in range(1, n):

        def their_step(c, _):
            rows = pl.ds(pl.multiple_of(c * chunk, chunk), chunk)
            outward(by, c).wait_recv()
            back[by - 1, rows, :] = mlp(theirs[by - 1, rows, :]).astype(BF16)
            homeward(by, c).start()
            return 0

        lax.fori_loop(0, chunks, their_step, 0)

    texts = chunk // seq

    def pool_step(c, _):
        rows = pl.ds(pl.multiple_of(c * chunk, chunk), chunk)
        out = total[rows, :]
        for by in range(1, n):
            homeward(by, c).wait_recv()
            out = out + parts[by - 1, rows, :].astype(F32)
        final = layer_norm(out, final_gain[...], final_bias[...])
        kept = keep[rows, :]
        summed = jnp.sum((final * kept).reshape(texts, seq, -1), axis=1)
        count = jnp.sum(kept.reshape(texts, seq, 1), axis=1)
        pooled[pl.ds(pl.multiple_of(c * texts, texts), texts), :] = summed / count
        return 0

    lax.fori_loop(0, chunks, pool_step, 0)
    loads[2].wait()
    emb = (
        jnp.dot(pooled[...].astype(BF16), head[...], preferred_element_type=F32) + head_bias[...]
    )
    unit[...] = unit_rows(emb).astype(BF16)
    for by in range(1, n):
        for c in range(chunks):
            outward(by, c).wait_send()
            homeward(by, c).wait_send()


def score_kernel(
    n,
    count,
    unit,
    images,
    teacher,
    scale_ref,
    offset_ref,
    grad,
    every,
    weights,
    side_send,
    side_recv,
    right_send,
    right_recv,
    left_send,
    left_recv,
    twin_send,
    twin_recv,
):
    dp = lax.axis_index("dp")
    me = lax.axis_index("fsdp")
    window, group, _ = teacher.shape
    texts = unit.shape[0]
    column = count // 4
    ring = 2 * column
    core = lax.rem(dp, 2)
    y = lax.rem(dp // 2, 2)
    z = dp // 4
    place = jnp.where(y == 0, z, ring - 1 - z)

    def at_place(p, c):
        p = lax.rem(p + 2 * ring, ring)
        return jnp.where(p < column, 4 * p, 4 * (ring - 1 - p) + 2) + c

    right = at_place(place + 1, core)
    left = at_place(place - 1, core)
    twin = dp + 1 - 2 * core
    friends = [(dp, lax.rem(me + by, n)) for by in range(1, n)]
    barrier = pltpu.get_barrier_semaphore()
    for other in friends + [(right, me), (left, me), (twin, me)]:
        pl.semaphore_signal(barrier, inc=1, device_id=other, device_id_type=MESH)

    mine = pl.ds(pl.multiple_of(me * texts, texts), texts)
    every[dp, mine, :] = unit[...]
    pl.semaphore_wait(barrier, n + 2)

    def copy(block, send, recv, to):
        return pltpu.make_async_remote_copy(
            src_ref=block,
            dst_ref=block,
            send_sem=send,
            recv_sem=recv,
            device_id=to,
            device_id_type=MESH,
        )

    sent = []

    def begin(block, send, recv, to):
        out = copy(block, send, recv, to)
        out.start()
        sent.append(out)

    for by in range(1, n):
        begin(every.at[dp, mine], side_send.at[by - 1], side_recv.at[by - 1], friends[by - 1])
    picture = unit_rows(images[...].astype(F32)).astype(BF16)
    weights[...] = jnp.zeros_like(weights)
    for by in range(1, n):
        source = lax.rem(me - by + n, n)
        rows = pl.ds(pl.multiple_of(source * texts, texts), texts)
        copy(
            every.at[dp, rows], side_send.at[by - 1], side_recv.at[by - 1], friends[by - 1]
        ).wait_recv()

    to_right = ring // 2
    to_left = ring - 1 - to_right
    twins = 0

    def to_twin(block):
        begin(block, twin_send.at[twins], twin_recv.at[twins], (twin, me))

    for step in range(to_right + 1):
        if step > 0:
            block = every.at[at_place(place - step, core)]
            copy(
                block, right_send.at[step - 1], right_recv.at[step - 1], (right, me)
            ).wait_recv()
        else:
            block = every.at[dp]
        if step < to_right:
            begin(block, right_send.at[step], right_recv.at[step], (right, me))
        if step < to_left and step == 0:
            begin(block, left_send.at[step], left_recv.at[step], (left, me))
        to_twin(block)
        twins += 1
        if 0 < step <= to_left:
            block = every.at[at_place(place + step, core)]
            copy(block, left_send.at[step - 1], left_recv.at[step - 1], (left, me)).wait_recv()
            if step < to_left:
                begin(block, left_send.at[step], left_recv.at[step], (left, me))
            to_twin(block)
            twins += 1
    twins = 0
    for step in range(to_right + 1):
        sources = [place - step]
        if 0 < step <= to_left:
            sources.append(place + step)
        for source in sources:
            copy(
                every.at[at_place(source, 1 - core)],
                twin_send.at[twins],
                twin_recv.at[twins],
                (twin, me),
            ).wait_recv()
            twins += 1

    scale = scale_ref[0]
    offset = offset_ref[0]

    def weigh(s, _):
        source = lax.rem(dp - s + count, count)
        score = (
            scale
            * lax.dot_general(
                every[source], picture, (((1,), (1,)), ((), ())), preferred_element_type=F32
            )
            + offset
        )
        weight = jax.nn.sigmoid(score) - jax.nn.sigmoid(teacher[s].astype(F32))
        weights[pl.ds(pl.multiple_of(source * group, group), group), :] = weight.astype(BF16)
        return 0

    lax.fori_loop(0, window, weigh, 0)
    grad[...] = scale * lax.dot_general(
        weights[...],
        every[...].reshape(count * group, every.shape[2]),
        (((0,), (0,)), ((), ())),
        preferred_element_type=F32,
    )
    for out in sent:
        out.wait_send()


def on_device(
    hidden,
    text_ids,
    ln_gain,
    ln_bias,
    fc1_weight,
    fc1_bias,
    fc2_weight,
    fc2_bias,
    final_gain,
    final_bias,
    head_weight,
    head_bias,
    image_emb,
    teacher_logits,
    logit_scale,
    logit_bias,
):
    tokens, width = hidden.shape
    texts, seq = text_ids.shape
    units = fc1_weight.shape[1]
    group, window, pictures = teacher_logits.shape
    n = lax.axis_size("fsdp")
    count = lax.axis_size("dp")
    me = lax.axis_index("fsdp")
    chunk = min(256, tokens)
    chunks = tokens // chunk
    others = max(n - 1, 1)

    slabs = jnp.transpose(teacher_logits, (1, 0, 2))
    tiles = [slabs[0]]
    for s in range(1, window):
        tiles.append(
            lax.ppermute(slabs[s], "dp", [(i, (i + s) % count) for i in range(count)])
        )
    tiles = jnp.stack(tiles)

    keep = (text_ids != 0).astype(F32).reshape(tokens, 1)
    bias_here = lax.dynamic_slice_in_dim(fc1_bias, me * units, units).reshape(1, units)
    vmem = pl.BlockSpec(memory_space=pltpu.VMEM)
    smem = pl.BlockSpec(memory_space=pltpu.SMEM)
    hbm = pl.BlockSpec(memory_space=pl.ANY)
    dma = pltpu.SemaphoreType.DMA
    row = lambda v: v.reshape(1, -1)
    flops = 4 * n * tokens * width * units
    unit = pl.pallas_call(
        functools.partial(mlp_kernel, n, chunk, 768, seq),
        out_shape=jax.ShapeDtypeStruct((texts, width), BF16),
        in_specs=[vmem, vmem, vmem, vmem, hbm, vmem, hbm, vmem, vmem, vmem, hbm, vmem],
        out_specs=vmem,
        scratch_shapes=[
            pltpu.VMEM(fc1_weight.shape, BF16),
            pltpu.VMEM(fc2_weight.shape, BF16),
            pltpu.VMEM(head_weight.shape, BF16),
            pltpu.VMEM((tokens, width), BF16),
            pltpu.VMEM((tokens, width), F32),
            pltpu.VMEM((others, tokens, width), BF16),
            pltpu.VMEM((others, tokens, width), BF16),
            pltpu.VMEM((others, tokens, width), BF16),
            pltpu.VMEM((texts, width), F32),
            dma((3,)),
            dma((others, chunks)),
            dma((others, chunks)),
            dma((others, chunks)),
            dma((others, chunks)),
        ],
        compiler_params=pltpu.CompilerParams(
            collective_id=0, has_side_effects=True, vmem_limit_bytes=60 * 1024 * 1024
        ),
        cost_estimate=pl.CostEstimate(
            flops=flops, bytes_accessed=4 * width * units, transcendentals=n * tokens * units
        ),
    )(
        hidden,
        keep,
        row(ln_gain),
        row(ln_bias),
        fc1_weight,
        bias_here,
        fc2_weight,
        row(fc2_bias),
        row(final_gain),
        row(final_bias),
        head_weight,
        row(head_bias),
    )
    ring = count // 2
    return pl.pallas_call(
        functools.partial(score_kernel, n, count),
        out_shape=jax.ShapeDtypeStruct((pictures, width), F32),
        in_specs=[vmem, vmem, vmem, smem, smem],
        out_specs=vmem,
        scratch_shapes=[
            pltpu.VMEM((count, group, width), BF16),
            pltpu.VMEM((count * group, pictures), BF16),
            dma((others,)),
            dma((others,)),
            dma((ring,)),
            dma((ring,)),
            dma((ring,)),
            dma((ring,)),
            dma((ring,)),
            dma((ring,)),
        ],
        compiler_params=pltpu.CompilerParams(
            collective_id=1, has_side_effects=True, vmem_limit_bytes=60 * 1024 * 1024
        ),
        cost_estimate=pl.CostEstimate(
            flops=4 * count * group * pictures * width,
            bytes_accessed=2 * count * group * width,
            transcendentals=2 * window * group * pictures,
        ),
    )(unit, image_emb, tiles, logit_scale, logit_bias)


def solution(mesh):
    placed = (
        P(("dp", "fsdp"), None),
        P(("dp", "fsdp"), None),
        P(),
        P(),
        P(None, "fsdp"),
        P(),
        P("fsdp", None),
        P(),
        P(),
        P(),
        P(),
        P(),
        P(("dp", "fsdp"), None),
        P("dp", None, "fsdp"),
        P(),
        P(),
    )
    return jax.shard_map(
        on_device, mesh=mesh, in_specs=placed, out_specs=P(("dp", "fsdp"), None), check_vma=False
    )
```

```python
import functools

import jax
import jax.numpy as jnp
from jax import lax
from jax.experimental import pallas as pl
from jax.experimental.pallas import tpu as pltpu
from jax.sharding import PartitionSpec as P

MESH = pl.DeviceIdType.MESH
F32 = jnp.float32
BF16 = jnp.bfloat16


def layer_norm(values, gain, shift):
    centre = jnp.mean(values, axis=-1, keepdims=True)
    moved = values - centre
    spread = jnp.mean(moved * moved, axis=-1, keepdims=True)
    return moved * lax.rsqrt(spread + 1e-06) * gain + shift


def unit_rows(values):
    return values * lax.rsqrt(jnp.sum(values * values, axis=-1, keepdims=True) + 1e-06)


def tower_kernel(
    n,
    count,
    tile,
    hidden,
    text_ids,
    ln_gain,
    ln_bias,
    fc1_hbm,
    fc1_bias,
    fc2_hbm,
    fc2_bias,
    final_gain,
    final_bias,
    head_hbm,
    head_bias,
    images,
    slabs,
    scale_ref,
    offset_ref,
    grad,
    fc1,
    fc2,
    head,
    normed,
    total,
    theirs,
    parts,
    every,
    tiles,
    load_sem,
    send_sem,
    recv_sem,
    back_send,
    back_recv,
    teach_send,
    teach_recv,
    side_send,
    side_recv,
    right_send,
    right_recv,
    left_send,
    left_recv,
    twin_send,
    twin_recv,
):
    dp = lax.axis_index("dp")
    me = lax.axis_index("fsdp")
    tokens, width = hidden.shape
    texts, seq = text_ids.shape
    units = fc1.shape[0]
    window = slabs.shape[0]
    phases, _, rows_here, _ = every.shape
    chunk = tokens // phases
    half = chunk // 2
    slots = texts // phases
    loads = [
        pltpu.make_async_copy(src, dst, load_sem.at[i])
        for i, (src, dst) in enumerate(((fc1_hbm, fc1), (fc2_hbm, fc2), (head_hbm, head)))
    ]
    for load in loads:
        load.start()

    column = count // 4
    ring = 2 * column
    core = lax.rem(dp, 2)
    y = lax.rem(dp // 2, 2)
    z = dp // 4
    place = jnp.where(y == 0, z, ring - 1 - z)

    def at_place(p, c):
        p = lax.rem(p + 2 * ring, ring)
        return jnp.where(p < column, 4 * p, 4 * (ring - 1 - p) + 2) + c

    right = at_place(place + 1, core)
    left = at_place(place - 1, core)
    twin = dp + 1 - 2 * core

    def ahead(by):
        return (dp, lax.rem(me + by + n, n))

    def later(s):
        return lax.rem(dp + s + count, count)

    tiles[...] = jnp.zeros_like(tiles)
    barrier = pltpu.get_barrier_semaphore()
    near = [ahead(by) for by in range(1, n)] + [(right, me), (left, me), (twin, me)]
    for other in near:
        pl.semaphore_signal(barrier, inc=1, device_id=other, device_id_type=MESH)

    def greet(s, _):
        pl.semaphore_signal(barrier, inc=1, device_id=(later(-s), me), device_id_type=MESH)
        return 0

    lax.fori_loop(1, window, greet, 0)

    def copy(src, dst, send, recv, to):
        return pltpu.make_async_remote_copy(
            src_ref=src, dst_ref=dst, send_sem=send, recv_sem=recv, device_id=to, device_id_type=MESH
        )

    def outward(by, c):
        rows = pl.ds(c * chunk, chunk)
        return copy(
            normed.at[rows],
            theirs.at[by - 1, rows],
            send_sem.at[by - 1, c],
            recv_sem.at[by - 1, c],
            ahead(by),
        )

    def homeward(by, c):
        rows = pl.ds(c * half, half)
        return copy(
            theirs.at[by - 1, rows],
            parts.at[by - 1, rows],
            back_send.at[by - 1, c],
            back_recv.at[by - 1, c],
            ahead(-by),
        )

    def lesson(s, block):
        return copy(slabs.at[s], tiles.at[block], teach_send.at[s], teach_recv.at[s], (later(s), me))

    def normalise(c):
        rows = pl.ds(c * chunk, chunk)
        normed[rows, :] = layer_norm(
            hidden[rows, :].astype(F32), ln_gain[...], ln_bias[...]
        ).astype(BF16)

    normalise(0)
    pl.semaphore_wait(barrier, n + 2 + window - 1)
    for c in range(phases):
        if c > 0:
            normalise(c)
        for by in range(1, n):
            outward(by, c).start()

    def teach(s, _):
        lesson(s, dp).start()
        return 0

    lax.fori_loop(1, window, teach, 0)
    tiles[dp] = slabs[0]
    picture = unit_rows(images[...].astype(F32)).astype(BF16)
    loads[0].wait()
    loads[1].wait()

    def mlp(values):
        mixed = None
        for low in range(0, units, tile):
            high = min(low + tile, units)
            pre = lax.dot_general(
                values, fc1[low:high, :], (((1,), (1,)), ((), ())), preferred_element_type=F32
            )
            bias = fc1_bias[pl.ds(me, 1), low:high]
            act = jax.nn.gelu(pre + bias, approximate=True).astype(BF16)
            term = jnp.dot(act, fc2[low:high, :], preferred_element_type=F32)
            mixed = term if mixed is None else mixed + term
        return mixed

    def own_step(c, _):
        rows = pl.ds(pl.multiple_of(c * chunk, chunk), chunk)
        total[rows, :] = mlp(normed[rows, :]) + hidden[rows, :].astype(F32) + fc2_bias[...]
        return 0

    lax.fori_loop(0, phases, own_step, 0)

    def their_step(c, _):
        rows = pl.ds(pl.multiple_of(c * chunk, chunk), chunk)
        for by in range(1, n):
            outward(by, c).wait_recv()

        def one(slot, _):
            theirs[slot, rows, :] = mlp(theirs[slot, rows, :]).astype(BF16)
            return 0

        lax.fori_loop(0, n - 1, one, 0)
        for by in range(1, n):
            homeward(by, 2 * c).start()

        @pl.when(c < phases - 1)
        def _():
            for by in range(1, n):
                homeward(by, 2 * c + 1).start()

        return 0

    lax.fori_loop(0, phases, their_step, 0)
    loads[2].wait()

    def embed(c):
        rows = pl.ds(c * chunk, chunk)
        out = total[rows, :]
        for by in range(1, n):
            homeward(by, 2 * c).wait_recv()
            homeward(by, 2 * c + 1).wait_recv()
            out = out + parts[by - 1, rows, :].astype(F32)
        final = layer_norm(out, final_gain[...], final_bias[...])
        kept = (text_ids[pl.ds(c * slots, slots), :] != 0).astype(F32)
        summed = jnp.sum(final.reshape(slots, seq, width) * kept[:, :, None], axis=1)
        pooled = summed / jnp.sum(kept, axis=1, keepdims=True)
        emb = (
            jnp.dot(pooled.astype(BF16), head[...], preferred_element_type=F32) + head_bias[...]
        )
        return unit_rows(emb).astype(BF16)

    sent = []

    def begin(block, send, recv, to):
        out = copy(block, block, send, recv, to)
        out.start()
        sent.append(out)

    def part(h, f):
        return every.at[h, dp, pl.ds(pl.multiple_of(f * slots, slots), slots)]

    def exchange(h):
        every[h, dp, pl.ds(pl.multiple_of(me * slots, slots), slots), :] = embed(h)
        for by in range(1, n):
            begin(part(h, me), side_send.at[h, by - 1], side_recv.at[h, by - 1], ahead(by))

    to_right = ring // 2
    to_left = ring - 1 - to_right

    def circulate(h):
        for by in range(1, n):
            block = part(h, lax.rem(me - by + n, n))
            copy(block, block, side_send.at[h, by - 1], side_recv.at[h, by - 1], ahead(by)).wait_recv()
        twins = 0
        for step in range(to_right + 1):
            block = every.at[h, at_place(place - step, core)]
            if step > 0:
                copy(
                    block, block, right_send.at[h, step - 1], right_recv.at[h, step - 1], (right, me)
                ).wait_recv()
            if step < to_right:
                begin(block, right_send.at[h, step], right_recv.at[h, step], (right, me))
            if step == 0 and to_left > 0:
                begin(block, left_send.at[h, 0], left_recv.at[h, 0], (left, me))
            begin(block, twin_send.at[h, twins], twin_recv.at[h, twins], (twin, me))
            twins += 1
            if 0 < step <= to_left:
                block = every.at[h, at_place(place + step, core)]
                copy(
                    block, block, left_send.at[h, step - 1], left_recv.at[h, step - 1], (left, me)
                ).wait_recv()
                if step < to_left:
                    begin(block, left_send.at[h, step], left_recv.at[h, step], (left, me))
                begin(block, twin_send.at[h, twins], twin_recv.at[h, twins], (twin, me))
                twins += 1
        twins = 0
        for step in range(to_right + 1):
            sources = [place - step]
            if 0 < step <= to_left:
                sources.append(place + step)
            for source in sources:
                block = every.at[h, at_place(source, 1 - core)]
                copy(
                    block, block, twin_send.at[h, twins], twin_recv.at[h, twins], (twin, me)
                ).wait_recv()
                twins += 1

    scale = scale_ref[0]
    offset = offset_ref[0]
    pictures = images.shape[0]
    span = (count, rows_here, pictures)
    behind = dp - lax.broadcasted_iota(jnp.int32, span, 0)
    met = jnp.where(behind < 0, behind + count, behind) < window

    def gradient(h):
        group = every[h].reshape(count * rows_here, width)
        dots = lax.dot_general(
            group, picture, (((1,), (1,)), ((), ())), preferred_element_type=F32
        )
        score = (scale * dots + offset).reshape(span)
        gap = jax.nn.sigmoid(score) - jax.nn.sigmoid(tiles[:, h].astype(F32))
        weight = jnp.where(met, gap, 0.0).astype(BF16).reshape(count * rows_here, pictures)
        return lax.dot_general(
            weight, group, (((0,), (0,)), ((), ())), preferred_element_type=F32
        )

    def taught(s, _):
        lesson(s, later(-s)).wait_recv()
        return 0

    for h in range(phases):
        exchange(h)
        if h == 0:
            for by in range(1, n):
                homeward(by, 2 * phases - 1).start()
        circulate(h)
        if h == 0:
            lax.fori_loop(1, window, taught, 0)
            grad[...] = gradient(h)
        else:
            grad[...] += gradient(h)
    grad[...] = scale * grad[...]

    def told(s, _):
        lesson(s, dp).wait_send()
        return 0

    lax.fori_loop(1, window, told, 0)
    for by in range(1, n):
        for c in range(phases):
            outward(by, c).wait_send()
        for c in range(2 * phases):
            homeward(by, c).wait_send()
    for out in sent:
        out.wait_send()


def on_device(
    hidden,
    text_ids,
    ln_gain,
    ln_bias,
    fc1_weight,
    fc1_bias,
    fc2_weight,
    fc2_bias,
    final_gain,
    final_bias,
    head_weight,
    head_bias,
    image_emb,
    teacher_logits,
    logit_scale,
    logit_bias,
):
    tokens, width = hidden.shape
    texts, seq = text_ids.shape
    units = fc1_weight.shape[1]
    group, window, pictures = teacher_logits.shape
    n = lax.axis_size("fsdp")
    count = lax.axis_size("dp")
    phases = 2
    slots = texts // phases
    others = max(n - 1, 1)

    slabs = jnp.transpose(
        teacher_logits.reshape(n, phases, slots, window, pictures), (3, 1, 0, 2, 4)
    ).reshape(window, phases, n * slots, pictures)
    vmem = pl.BlockSpec(memory_space=pltpu.VMEM)
    smem = pl.BlockSpec(memory_space=pltpu.SMEM)
    hbm = pl.BlockSpec(memory_space=pl.ANY)
    dma = pltpu.SemaphoreType.DMA
    ring = count // 2
    return pl.pallas_call(
        functools.partial(tower_kernel, n, count, 768),
        out_shape=jax.ShapeDtypeStruct((pictures, width), F32),
        in_specs=[vmem] * 4 + [hbm, vmem, hbm, vmem, vmem, vmem, hbm, vmem, vmem, vmem, smem, smem],
        out_specs=vmem,
        scratch_shapes=[
            pltpu.VMEM((units, width), BF16),
            pltpu.VMEM(fc2_weight.shape, BF16),
            pltpu.VMEM(head_weight.shape, BF16),
            pltpu.VMEM((tokens, width), BF16),
            pltpu.VMEM((tokens, width), F32),
            pltpu.VMEM((others, tokens, width), BF16),
            pltpu.VMEM((others, tokens, width), BF16),
            pltpu.VMEM((phases, count, n * slots, width), BF16),
            pltpu.VMEM((count, phases, n * slots, pictures), BF16),
            dma((3,)),
            dma((others, phases)),
            dma((others, phases)),
            dma((others, 2 * phases)),
            dma((others, 2 * phases)),
            dma((window,)),
            dma((window,)),
            dma((phases, others)),
            dma((phases, others)),
        ]
        + [dma((phases, ring))] * 6,
        compiler_params=pltpu.CompilerParams(
            collective_id=0, has_side_effects=True, vmem_limit_bytes=62 * 1024 * 1024
        ),
        cost_estimate=pl.CostEstimate(
            flops=4 * n * tokens * width * units,
            bytes_accessed=4 * width * units,
            transcendentals=n * tokens * units,
        ),
    )(
        hidden,
        text_ids,
        ln_gain,
        ln_bias,
        fc1_weight.T,
        fc1_bias.reshape(n, units),
        fc2_weight,
        fc2_bias,
        final_gain,
        final_bias,
        head_weight,
        head_bias,
        image_emb,
        slabs,
        logit_scale,
        logit_bias,
    )


def solution(mesh):
    placed = (
        P(("dp", "fsdp"), None),
        P(("dp", "fsdp"), None),
        P(),
        P(),
        P(None, "fsdp"),
        P(),
        P("fsdp", None),
        P(),
        P(),
        P(),
        P(),
        P(),
        P(("dp", "fsdp"), None),
        P("dp", None, "fsdp"),
        P(),
        P(),
    )
    return jax.shard_map(
        on_device, mesh=mesh, in_specs=placed, out_specs=P(("dp", "fsdp"), None), check_vma=False
    )
```

```python
import functools

import jax
import jax.numpy as jnp
from jax import lax
from jax.experimental import pallas as pl
from jax.experimental.pallas import tpu as pltpu
from jax.sharding import PartitionSpec as P

MESH = pl.DeviceIdType.MESH
F32 = jnp.float32
BF16 = jnp.bfloat16


def layer_norm(values, gain, shift):
    centre = jnp.mean(values, axis=-1, keepdims=True)
    moved = values - centre
    spread = jnp.mean(moved * moved, axis=-1, keepdims=True)
    return moved * lax.rsqrt(spread + 1e-06) * gain + shift


def unit_rows(values):
    return values * lax.rsqrt(jnp.sum(values * values, axis=-1, keepdims=True) + 1e-06)


def tower_kernel(
    n,
    count,
    tile,
    hidden,
    text_ids,
    ln_gain,
    ln_bias,
    fc1_hbm,
    fc1_bias,
    fc2_hbm,
    fc2_bias,
    final_gain,
    final_bias,
    head_hbm,
    head_bias,
    images,
    teacher,
    scale_ref,
    offset_ref,
    grad,
    slabs,
    bias,
    kept_rows,
    fc1,
    fc2,
    head,
    normed,
    total,
    theirs,
    parts,
    every,
    tiles,
    load_sem,
    send_sem,
    recv_sem,
    back_send,
    back_recv,
    teach_send,
    teach_recv,
    side_send,
    side_recv,
    right_send,
    right_recv,
    left_send,
    left_recv,
    twin_send,
    twin_recv,
):
    dp = lax.axis_index("dp")
    me = lax.axis_index("fsdp")
    tokens, width = hidden.shape
    seq, texts = text_ids.shape
    units = fc1.shape[0]
    window = slabs.shape[0]
    phases, _, rows_here, _ = every.shape
    chunk = tokens // phases
    quarter = chunk // 2
    quarters = 2 * phases
    slots = texts // phases
    loads = [
        pltpu.make_async_copy(src, dst, load_sem.at[i])
        for i, (src, dst) in enumerate(((fc1_hbm, fc1), (fc2_hbm, fc2), (head_hbm, head)))
    ]
    for load in loads:
        load.start()

    column = count // 4
    ring = 2 * column
    core = lax.rem(dp, 2)
    y = lax.rem(dp // 2, 2)
    z = dp // 4
    place = jnp.where(y == 0, z, ring - 1 - z)

    def at_place(p, c):
        p = lax.rem(p + 2 * ring, ring)
        return jnp.where(p < column, 4 * p, 4 * (ring - 1 - p) + 2) + c

    right = at_place(place + 1, core)
    left = at_place(place - 1, core)
    twin = dp + 1 - 2 * core

    def ahead(by):
        return (dp, lax.rem(me + by + n, n))

    def later(s):
        return lax.rem(dp + s + count, count)

    tiles[...] = jnp.zeros_like(tiles)
    barrier = pltpu.get_barrier_semaphore()
    near = [ahead(by) for by in range(1, n)] + [(right, me), (left, me), (twin, me)]
    for other in near:
        pl.semaphore_signal(barrier, inc=1, device_id=other, device_id_type=MESH)

    def greet(s, _):
        pl.semaphore_signal(barrier, inc=1, device_id=(later(-s), me), device_id_type=MESH)
        return 0

    lax.fori_loop(1, window, greet, 0)

    def copy(src, dst, send, recv, to):
        return pltpu.make_async_remote_copy(
            src_ref=src, dst_ref=dst, send_sem=send, recv_sem=recv, device_id=to, device_id_type=MESH
        )

    def outward(by, c):
        rows = pl.ds(c * quarter, quarter)
        return copy(
            normed.at[rows],
            theirs.at[by - 1, rows],
            send_sem.at[by - 1, c],
            recv_sem.at[by - 1, c],
            ahead(by),
        )

    def homeward(by, c):
        rows = pl.ds(c * quarter, quarter)
        return copy(
            theirs.at[by - 1, rows],
            parts.at[by - 1, rows],
            back_send.at[by - 1, c],
            back_recv.at[by - 1, c],
            ahead(-by),
        )

    def lesson(s, block):
        return copy(slabs.at[s], tiles.at[block], teach_send.at[s], teach_recv.at[s], (later(s), me))

    def normalise(c):
        rows = pl.ds(c * chunk, chunk)
        normed[rows, :] = layer_norm(
            hidden[rows, :].astype(F32), ln_gain[...], ln_bias[...]
        ).astype(BF16)

    def go_out(c):
        for by in range(1, n):
            outward(by, c).start()

    def go_home(c):
        for by in range(1, n):
            homeward(by, c).start()

    normalise(0)
    pl.semaphore_wait(barrier, n + 2 + window - 1)
    go_out(0)
    go_out(1)

    def teach(s, _):
        turned = teacher[s].astype(F32).T
        for f in range(n):
            for h in range(phases):
                low = (f * phases + h) * slots
                slabs[s, h, f * slots : (f + 1) * slots, :] = turned[low : low + slots].astype(
                    BF16
                )

        @pl.when(s > 0)
        def _():
            lesson(s, dp).start()

        return 0

    lax.fori_loop(0, window, teach, 0)
    tiles[dp] = slabs[0]
    for c in range(1, phases):
        normalise(c)
    for f in range(n):

        @pl.when(me == f)
        def _():
            bias[...] = fc1_bias[f * units : (f + 1) * units].reshape(1, units)

    kept_rows[...] = (text_ids[...] != 0).astype(F32).T
    picture = unit_rows(images[...].astype(F32)).astype(BF16)
    loads[0].wait()
    loads[1].wait()

    def mlp(values):
        mixed = None
        for low in range(0, units, tile):
            high = min(low + tile, units)
            pre = lax.dot_general(
                values, fc1[low:high, :], (((1,), (1,)), ((), ())), preferred_element_type=F32
            )
            act = jax.nn.gelu(pre + bias[:, low:high], approximate=True).astype(BF16)
            term = jnp.dot(act, fc2[low:high, :], preferred_element_type=F32)
            mixed = term if mixed is None else mixed + term
        return mixed

    def own(c):
        rows = pl.ds(c * chunk, chunk)
        total[rows, :] = mlp(normed[rows, :]) + hidden[rows, :].astype(F32) + fc2_bias[...]

    def their(c):
        rows = pl.ds(pl.multiple_of(c * quarter, quarter), quarter)
        for by in range(1, n):
            outward(by, c).wait_recv()

        def one(slot, _):
            theirs[slot, rows, :] = mlp(theirs[slot, rows, :]).astype(BF16)
            return 0

        lax.fori_loop(0, n - 1, one, 0)

    def early(c, _):
        their(c)
        go_home(c)
        go_out(c + 2)
        return 0

    own(0)
    lax.fori_loop(0, 2, early, 0)
    own(1)
    their(2)
    loads[2].wait()

    def embed(c):
        rows = pl.ds(c * chunk, chunk)
        out = total[rows, :]
        for by in range(1, n):
            homeward(by, 2 * c).wait_recv()
            homeward(by, 2 * c + 1).wait_recv()
            out = out + parts[by - 1, rows, :].astype(F32)
        final = layer_norm(out, final_gain[...], final_bias[...])
        kept = kept_rows[pl.ds(c * slots, slots), :]
        summed = jnp.sum(final.reshape(slots, seq, width) * kept[:, :, None], axis=1)
        pooled = summed / jnp.sum(kept, axis=1, keepdims=True)
        emb = (
            jnp.dot(pooled.astype(BF16), head[...], preferred_element_type=F32) + head_bias[...]
        )
        return unit_rows(emb).astype(BF16)

    sent = []

    def begin(block, send, recv, to):
        out = copy(block, block, send, recv, to)
        out.start()
        sent.append(out)

    def part(h, f):
        return every.at[h, dp, pl.ds(pl.multiple_of(f * slots, slots), slots)]

    def exchange(h):
        every[h, dp, pl.ds(pl.multiple_of(me * slots, slots), slots), :] = embed(h)
        for by in range(1, n):
            begin(part(h, me), side_send.at[h, by - 1], side_recv.at[h, by - 1], ahead(by))

    to_right = ring // 2
    to_left = ring - 1 - to_right

    def side_in(h):
        for by in range(1, n):
            block = part(h, lax.rem(me - by + n, n))
            copy(block, block, side_send.at[h, by - 1], side_recv.at[h, by - 1], ahead(by)).wait_recv()

    def set_off(h):
        block = every.at[h, dp]
        begin(block, right_send.at[h, 0], right_recv.at[h, 0], (right, me))
        if to_left > 0:
            begin(block, left_send.at[h, 0], left_recv.at[h, 0], (left, me))
        begin(block, twin_send.at[h, 0], twin_recv.at[h, 0], (twin, me))

    def circulate(h):
        twins = 1
        for step in range(1, to_right + 1):
            block = every.at[h, at_place(place - step, core)]
            copy(
                block, block, right_send.at[h, step - 1], right_recv.at[h, step - 1], (right, me)
            ).wait_recv()
            if step < to_right:
                begin(block, right_send.at[h, step], right_recv.at[h, step], (right, me))
            begin(block, twin_send.at[h, twins], twin_recv.at[h, twins], (twin, me))
            twins += 1
            if step <= to_left:
                block = every.at[h, at_place(place + step, core)]
                copy(
                    block, block, left_send.at[h, step - 1], left_recv.at[h, step - 1], (left, me)
                ).wait_recv()
                if step < to_left:
                    begin(block, left_send.at[h, step], left_recv.at[h, step], (left, me))
                begin(block, twin_send.at[h, twins], twin_recv.at[h, twins], (twin, me))
                twins += 1
        twins = 0
        for step in range(to_right + 1):
            sources = [place - step]
            if 0 < step <= to_left:
                sources.append(place + step)
            for source in sources:
                block = every.at[h, at_place(source, 1 - core)]
                copy(
                    block, block, twin_send.at[h, twins], twin_recv.at[h, twins], (twin, me)
                ).wait_recv()
                twins += 1

    scale = scale_ref[0]
    offset = offset_ref[0]
    pictures = images.shape[0]
    span = (count, rows_here, pictures)
    behind = dp - lax.broadcasted_iota(jnp.int32, span, 0)
    met = jnp.where(behind < 0, behind + count, behind) < window

    def gradient(h):
        group = every[h].reshape(count * rows_here, width)
        dots = lax.dot_general(
            group, picture, (((1,), (1,)), ((), ())), preferred_element_type=F32
        )
        score = (scale * dots + offset).reshape(span)
        gap = jax.nn.sigmoid(score) - jax.nn.sigmoid(tiles[:, h].astype(F32))
        weight = jnp.where(met, gap, 0.0).astype(BF16).reshape(count * rows_here, pictures)
        return lax.dot_general(
            weight, group, (((0,), (0,)), ((), ())), preferred_element_type=F32
        )

    def taught(s, _):
        lesson(s, later(-s)).wait_recv()
        return 0

    exchange(0)
    go_home(2)
    side_in(0)
    set_off(0)
    their(3)
    go_home(3)
    circulate(0)
    lax.fori_loop(1, window, taught, 0)
    grad[...] = gradient(0)
    exchange(1)
    side_in(1)
    set_off(1)
    circulate(1)
    grad[...] += gradient(1)

    def told(s, _):
        lesson(s, dp).wait_send()
        return 0

    lax.fori_loop(1, window, told, 0)
    for by in range(1, n):
        for c in range(quarters):
            outward(by, c).wait_send()
            homeward(by, c).wait_send()
    for out in sent:
        out.wait_send()


def on_device(
    hidden,
    text_ids,
    ln_gain,
    ln_bias,
    fc1_weight,
    fc1_bias,
    fc2_weight,
    fc2_bias,
    final_gain,
    final_bias,
    head_weight,
    head_bias,
    image_emb,
    teacher_logits,
    logit_scale,
    logit_bias,
):
    tokens, width = hidden.shape
    texts = text_ids.shape[0]
    units = fc1_weight.shape[1]
    group, window, pictures = teacher_logits.shape
    n = lax.axis_size("fsdp")
    count = lax.axis_size("dp")
    phases = 2
    slots = texts // phases
    others = max(n - 1, 1)

    vmem = pl.BlockSpec(memory_space=pltpu.VMEM)
    smem = pl.BlockSpec(memory_space=pltpu.SMEM)
    hbm = pl.BlockSpec(memory_space=pl.ANY)
    dma = pltpu.SemaphoreType.DMA
    ring = count // 2
    total = pl.pallas_call(
        functools.partial(tower_kernel, n, count, 768),
        out_shape=jax.ShapeDtypeStruct((pictures, width), F32),
        in_specs=[vmem] * 4 + [hbm, vmem, hbm, vmem, vmem, vmem, hbm, vmem, vmem, vmem, smem, smem],
        out_specs=vmem,
        scratch_shapes=[
            pltpu.VMEM((window, phases, n * slots, pictures), BF16),
            pltpu.VMEM((1, units), F32),
            pltpu.VMEM((texts, text_ids.shape[1]), F32),
            pltpu.VMEM((units, width), BF16),
            pltpu.VMEM(fc2_weight.shape, BF16),
            pltpu.VMEM(head_weight.shape, BF16),
            pltpu.VMEM((tokens, width), BF16),
            pltpu.VMEM((tokens, width), F32),
            pltpu.VMEM((others, tokens, width), BF16),
            pltpu.VMEM((others, tokens, width), BF16),
            pltpu.VMEM((phases, count, n * slots, width), BF16),
            pltpu.VMEM((count, phases, n * slots, pictures), BF16),
            dma((3,)),
            dma((others, 2 * phases)),
            dma((others, 2 * phases)),
            dma((others, 2 * phases)),
            dma((others, 2 * phases)),
            dma((window,)),
            dma((window,)),
            dma((phases, others)),
            dma((phases, others)),
        ]
        + [dma((phases, ring))] * 6,
        compiler_params=pltpu.CompilerParams(
            collective_id=0, has_side_effects=True, vmem_limit_bytes=62 * 1024 * 1024
        ),
        cost_estimate=pl.CostEstimate(
            flops=4 * n * tokens * width * units,
            bytes_accessed=4 * width * units,
            transcendentals=n * tokens * units,
        ),
    )(
        hidden,
        text_ids.T,
        ln_gain,
        ln_bias,
        fc1_weight.T,
        fc1_bias,
        fc2_weight,
        fc2_bias,
        final_gain,
        final_bias,
        head_weight,
        head_bias,
        image_emb,
        jnp.transpose(teacher_logits, (1, 2, 0)),
        logit_scale,
        logit_bias,
    )
    return logit_scale[0] * total


def solution(mesh):
    placed = (
        P(("dp", "fsdp"), None),
        P(("dp", "fsdp"), None),
        P(),
        P(),
        P(None, "fsdp"),
        P(),
        P("fsdp", None),
        P(),
        P(),
        P(),
        P(),
        P(),
        P(("dp", "fsdp"), None),
        P("dp", None, "fsdp"),
        P(),
        P(),
    )
    return jax.shard_map(
        on_device, mesh=mesh, in_specs=placed, out_specs=P(("dp", "fsdp"), None), check_vma=False
    )
```

```python
import functools

import jax
import jax.numpy as jnp
from jax import lax
from jax.experimental import pallas as pl
from jax.experimental.pallas import tpu as pltpu
from jax.sharding import PartitionSpec as P

MESH = pl.DeviceIdType.MESH
F32 = jnp.float32
BF16 = jnp.bfloat16


def layer_norm(values, gain, shift):
    centre = jnp.mean(values, axis=-1, keepdims=True)
    moved = values - centre
    spread = jnp.mean(moved * moved, axis=-1, keepdims=True)
    return moved * lax.rsqrt(spread + 1e-06) * gain + shift


def unit_rows(values):
    return values * lax.rsqrt(jnp.sum(values * values, axis=-1, keepdims=True) + 1e-06)


def tower_kernel(
    n,
    count,
    tile,
    hidden,
    text_ids,
    ln_gain,
    ln_bias,
    fc1_hbm,
    fc1_bias,
    fc2_hbm,
    fc2_bias,
    final_gain,
    final_bias,
    head_hbm,
    head_bias,
    images,
    teacher,
    scale_ref,
    offset_ref,
    grad,
    slabs,
    bias,
    kept_rows,
    fc1,
    fc2,
    head,
    normed,
    total,
    theirs,
    parts,
    every,
    tiles,
    load_sem,
    send_sem,
    recv_sem,
    back_send,
    back_recv,
    teach_send,
    teach_recv,
    side_send,
    side_recv,
    right_send,
    right_recv,
    left_send,
    left_recv,
    twin_send,
    twin_recv,
):
    dp = lax.axis_index("dp")
    me = lax.axis_index("fsdp")
    tokens, width = hidden.shape
    seq, texts = text_ids.shape
    units = fc1.shape[0]
    window = slabs.shape[0]
    phases, _, pairs, rows_here, _ = every.shape
    chunk = tokens // phases
    quarter = chunk // 2
    quarters = 2 * phases
    slots = texts // phases
    loads = [
        pltpu.make_async_copy(src, dst, load_sem.at[i])
        for i, (src, dst) in enumerate(((fc1_hbm, fc1), (fc2_hbm, fc2), (head_hbm, head)))
    ]
    for load in loads:
        load.start()

    column = count // 4
    ring = 2 * column
    core = lax.rem(dp, 2)
    y = lax.rem(dp // 2, 2)
    z = dp // 4
    place = jnp.where(y == 0, z, ring - 1 - z)

    def at_place(p, c):
        p = lax.rem(p + 2 * ring, ring)
        return jnp.where(p < column, 4 * p, 4 * (ring - 1 - p) + 2) + c

    right = at_place(place + 1, core)
    left = at_place(place - 1, core)
    twin = dp + 1 - 2 * core

    def ahead(by):
        return (dp, lax.rem(me + by + n, n))

    def later(s):
        return lax.rem(dp + s + count, count)

    tiles[...] = jnp.zeros_like(tiles)
    barrier = pltpu.get_barrier_semaphore()
    near = [ahead(by) for by in range(1, n)] + [(right, me), (left, me), (twin, me)]
    for other in near:
        pl.semaphore_signal(barrier, inc=1, device_id=other, device_id_type=MESH)

    def greet(s, _):
        pl.semaphore_signal(barrier, inc=1, device_id=(later(-s), me), device_id_type=MESH)
        return 0

    lax.fori_loop(1, window, greet, 0)

    def copy(src, dst, send, recv, to):
        return pltpu.make_async_remote_copy(
            src_ref=src, dst_ref=dst, send_sem=send, recv_sem=recv, device_id=to, device_id_type=MESH
        )

    def outward(by, c):
        rows = pl.ds(c * quarter, quarter)
        return copy(
            normed.at[rows],
            theirs.at[by - 1, rows],
            send_sem.at[by - 1, c],
            recv_sem.at[by - 1, c],
            ahead(by),
        )

    def homeward(by, c):
        rows = pl.ds(c * quarter, quarter)
        return copy(
            theirs.at[by - 1, rows],
            parts.at[by - 1, rows],
            back_send.at[by - 1, c],
            back_recv.at[by - 1, c],
            ahead(-by),
        )

    def lesson(s, block):
        return copy(slabs.at[s], tiles.at[lax.rem(block, 2), block // 2], teach_send.at[s], teach_recv.at[s], (later(s), me))

    def normalise(c):
        rows = pl.ds(c * chunk, chunk)
        normed[rows, :] = layer_norm(
            hidden[rows, :].astype(F32), ln_gain[...], ln_bias[...]
        ).astype(BF16)

    def go_out(c):
        for by in range(1, n):
            outward(by, c).start()

    def go_home(c):
        for by in range(1, n):
            homeward(by, c).start()

    normalise(0)
    pl.semaphore_wait(barrier, n + 2 + window - 1)
    go_out(0)
    go_out(1)

    def teach(s, _):
        turned = teacher[s].astype(F32).T
        for f in range(n):
            for h in range(phases):
                low = (f * phases + h) * slots
                slabs[s, h, f * slots : (f + 1) * slots, :] = turned[low : low + slots].astype(
                    BF16
                )

        @pl.when(s > 0)
        def _():
            lesson(s, dp).start()

        return 0

    lax.fori_loop(0, window, teach, 0)
    tiles[core, dp // 2] = slabs[0]
    for c in range(1, phases):
        normalise(c)
    for f in range(n):

        @pl.when(me == f)
        def _():
            bias[...] = fc1_bias[f * units : (f + 1) * units].reshape(1, units)

    kept_rows[...] = (text_ids[...] != 0).astype(F32).T
    picture = unit_rows(images[...].astype(F32)).astype(BF16)
    loads[0].wait()
    loads[1].wait()

    def mlp(values):
        mixed = None
        for low in range(0, units, tile):
            high = min(low + tile, units)
            pre = lax.dot_general(
                values, fc1[low:high, :], (((1,), (1,)), ((), ())), preferred_element_type=F32
            )
            act = jax.nn.gelu(pre + bias[:, low:high], approximate=True).astype(BF16)
            term = jnp.dot(act, fc2[low:high, :], preferred_element_type=F32)
            mixed = term if mixed is None else mixed + term
        return mixed

    def own(c):
        rows = pl.ds(c * chunk, chunk)
        total[rows, :] = mlp(normed[rows, :]) + hidden[rows, :].astype(F32) + fc2_bias[...]

    def their(c):
        rows = pl.ds(pl.multiple_of(c * quarter, quarter), quarter)
        for by in range(1, n):
            outward(by, c).wait_recv()

        def one(slot, _):
            theirs[slot, rows, :] = mlp(theirs[slot, rows, :]).astype(BF16)
            return 0

        lax.fori_loop(0, n - 1, one, 0)

    def early(c, _):
        their(c)
        go_home(c)
        go_out(c + 2)
        return 0

    own(0)
    lax.fori_loop(0, 2, early, 0)
    own(1)
    their(2)
    loads[2].wait()

    def embed(c):
        rows = pl.ds(c * chunk, chunk)
        out = total[rows, :]
        for by in range(1, n):
            homeward(by, 2 * c).wait_recv()
            homeward(by, 2 * c + 1).wait_recv()
            out = out + parts[by - 1, rows, :].astype(F32)
        final = layer_norm(out, final_gain[...], final_bias[...])
        kept = kept_rows[pl.ds(c * slots, slots), :]
        summed = jnp.sum(final.reshape(slots, seq, width) * kept[:, :, None], axis=1)
        pooled = summed / jnp.sum(kept, axis=1, keepdims=True)
        emb = (
            jnp.dot(pooled.astype(BF16), head[...], preferred_element_type=F32) + head_bias[...]
        )
        return unit_rows(emb).astype(BF16)

    sent = []

    def begin(block, send, recv, to):
        out = copy(block, block, send, recv, to)
        out.start()
        sent.append(out)

    def part(h, f):
        return every.at[h, core, dp // 2, pl.ds(pl.multiple_of(f * slots, slots), slots)]

    def exchange(h):
        every[h, core, dp // 2, pl.ds(pl.multiple_of(me * slots, slots), slots), :] = embed(h)
        for by in range(1, n):
            begin(part(h, me), side_send.at[h, by - 1], side_recv.at[h, by - 1], ahead(by))

    to_right = ring // 2
    to_left = ring - 1 - to_right

    def side_in(h):
        for by in range(1, n):
            block = part(h, lax.rem(me - by + n, n))
            copy(block, block, side_send.at[h, by - 1], side_recv.at[h, by - 1], ahead(by)).wait_recv()

    def set_off(h):
        block = every.at[h, core, dp // 2]
        begin(block, right_send.at[h, 0], right_recv.at[h, 0], (right, me))
        if to_left > 0:
            begin(block, left_send.at[h, 0], left_recv.at[h, 0], (left, me))
        begin(block, twin_send.at[h, 0], twin_recv.at[h, 0], (twin, me))

    def circulate(h):
        twins = 1
        for step in range(1, to_right + 1):
            block = every.at[h, core, at_place(place - step, 0) // 2]
            copy(
                block, block, right_send.at[h, step - 1], right_recv.at[h, step - 1], (right, me)
            ).wait_recv()
            if step < to_right:
                begin(block, right_send.at[h, step], right_recv.at[h, step], (right, me))
            begin(block, twin_send.at[h, twins], twin_recv.at[h, twins], (twin, me))
            twins += 1
            if step <= to_left:
                block = every.at[h, core, at_place(place + step, 0) // 2]
                copy(
                    block, block, left_send.at[h, step - 1], left_recv.at[h, step - 1], (left, me)
                ).wait_recv()
                if step < to_left:
                    begin(block, left_send.at[h, step], left_recv.at[h, step], (left, me))
                begin(block, twin_send.at[h, twins], twin_recv.at[h, twins], (twin, me))
                twins += 1

    def twins_in(h):
        twins = 0
        for step in range(to_right + 1):
            sources = [place - step]
            if 0 < step <= to_left:
                sources.append(place + step)
            for source in sources:
                block = every.at[h, 1 - core, at_place(source, 0) // 2]
                copy(
                    block, block, twin_send.at[h, twins], twin_recv.at[h, twins], (twin, me)
                ).wait_recv()
                twins += 1

    scale = scale_ref[0]
    offset = offset_ref[0]
    pictures = images.shape[0]
    span = (pairs, rows_here, pictures)
    pair = lax.broadcasted_iota(jnp.int32, span, 0)

    def gradient(h, side):
        group = every[h, side].reshape(pairs * rows_here, width)
        dots = lax.dot_general(
            group, picture, (((1,), (1,)), ((), ())), preferred_element_type=F32
        )
        score = (scale * dots + offset).reshape(span)
        gap = jax.nn.sigmoid(score) - jax.nn.sigmoid(tiles[side, :, h].astype(F32))
        behind = dp - side - 2 * pair
        met = jnp.where(behind < 0, behind + count, behind) < window
        weight = jnp.where(met, gap, 0.0).astype(BF16).reshape(pairs * rows_here, pictures)
        return lax.dot_general(
            weight, group, (((0,), (0,)), ((), ())), preferred_element_type=F32
        )

    def taught(s, _):
        lesson(s, later(-s)).wait_recv()
        return 0

    exchange(0)
    go_home(2)
    side_in(0)
    set_off(0)
    their(3)
    go_home(3)
    circulate(0)
    twins_in(0)
    lax.fori_loop(1, window, taught, 0)
    exchange(1)
    grad[...] = gradient(0, core) + gradient(0, 1 - core)
    side_in(1)
    set_off(1)
    circulate(1)
    grad[...] += gradient(1, core)
    twins_in(1)
    grad[...] += gradient(1, 1 - core)

    def told(s, _):
        lesson(s, dp).wait_send()
        return 0

    lax.fori_loop(1, window, told, 0)
    for by in range(1, n):
        for c in range(quarters):
            outward(by, c).wait_send()
            homeward(by, c).wait_send()
    for out in sent:
        out.wait_send()


def on_device(
    hidden,
    text_ids,
    ln_gain,
    ln_bias,
    fc1_weight,
    fc1_bias,
    fc2_weight,
    fc2_bias,
    final_gain,
    final_bias,
    head_weight,
    head_bias,
    image_emb,
    teacher_logits,
    logit_scale,
    logit_bias,
):
    tokens, width = hidden.shape
    texts = text_ids.shape[0]
    units = fc1_weight.shape[1]
    group, window, pictures = teacher_logits.shape
    n = lax.axis_size("fsdp")
    count = lax.axis_size("dp")
    phases = 2
    slots = texts // phases
    others = max(n - 1, 1)

    vmem = pl.BlockSpec(memory_space=pltpu.VMEM)
    smem = pl.BlockSpec(memory_space=pltpu.SMEM)
    hbm = pl.BlockSpec(memory_space=pl.ANY)
    dma = pltpu.SemaphoreType.DMA
    ring = count // 2
    total = pl.pallas_call(
        functools.partial(tower_kernel, n, count, 768),
        out_shape=jax.ShapeDtypeStruct((pictures, width), F32),
        in_specs=[vmem] * 4 + [hbm, vmem, hbm, vmem, vmem, vmem, hbm, vmem, vmem, vmem, smem, smem],
        out_specs=vmem,
        scratch_shapes=[
            pltpu.VMEM((window, phases, n * slots, pictures), BF16),
            pltpu.VMEM((1, units), F32),
            pltpu.VMEM((texts, text_ids.shape[1]), F32),
            pltpu.VMEM((units, width), BF16),
            pltpu.VMEM(fc2_weight.shape, BF16),
            pltpu.VMEM(head_weight.shape, BF16),
            pltpu.VMEM((tokens, width), BF16),
            pltpu.VMEM((tokens, width), F32),
            pltpu.VMEM((others, tokens, width), BF16),
            pltpu.VMEM((others, tokens, width), BF16),
            pltpu.VMEM((phases, 2, count // 2, n * slots, width), BF16),
            pltpu.VMEM((2, count // 2, phases, n * slots, pictures), BF16),
            dma((3,)),
            dma((others, 2 * phases)),
            dma((others, 2 * phases)),
            dma((others, 2 * phases)),
            dma((others, 2 * phases)),
            dma((window,)),
            dma((window,)),
            dma((phases, others)),
            dma((phases, others)),
        ]
        + [dma((phases, ring))] * 6,
        compiler_params=pltpu.CompilerParams(
            collective_id=0, has_side_effects=True, vmem_limit_bytes=62 * 1024 * 1024
        ),
        cost_estimate=pl.CostEstimate(
            flops=4 * n * tokens * width * units,
            bytes_accessed=4 * width * units,
            transcendentals=n * tokens * units,
        ),
    )(
        hidden,
        text_ids.T,
        ln_gain,
        ln_bias,
        fc1_weight.T,
        fc1_bias,
        fc2_weight,
        fc2_bias,
        final_gain,
        final_bias,
        head_weight,
        head_bias,
        image_emb,
        jnp.transpose(teacher_logits, (1, 2, 0)),
        logit_scale,
        logit_bias,
    )
    return logit_scale[0] * total


def solution(mesh):
    placed = (
        P(("dp", "fsdp"), None),
        P(("dp", "fsdp"), None),
        P(),
        P(),
        P(None, "fsdp"),
        P(),
        P("fsdp", None),
        P(),
        P(),
        P(),
        P(),
        P(),
        P(("dp", "fsdp"), None),
        P("dp", None, "fsdp"),
        P(),
        P(),
    )
    return jax.shard_map(
        on_device, mesh=mesh, in_specs=placed, out_specs=P(("dp", "fsdp"), None), check_vma=False
    )
```

```python
import functools

import jax
import jax.numpy as jnp
from jax import lax
from jax.experimental import pallas as pl
from jax.experimental.pallas import tpu as pltpu
from jax.sharding import PartitionSpec as P

MESH = pl.DeviceIdType.MESH
F32 = jnp.float32
BF16 = jnp.bfloat16


def layer_norm(values, gain, shift):
    centre = jnp.mean(values, axis=-1, keepdims=True)
    moved = values - centre
    spread = jnp.mean(moved * moved, axis=-1, keepdims=True)
    return moved * lax.rsqrt(spread + 1e-06) * gain + shift


def unit_rows(values):
    return values * lax.rsqrt(jnp.sum(values * values, axis=-1, keepdims=True) + 1e-06)


def tower_kernel(
    n,
    count,
    tile,
    hidden,
    text_ids,
    ln_gain,
    ln_bias,
    fc1_hbm,
    fc1_bias,
    fc2_hbm,
    fc2_bias,
    final_gain,
    final_bias,
    head_hbm,
    head_bias,
    images,
    teacher,
    scale_ref,
    offset_ref,
    grad,
    slabs,
    bias,
    kept_rows,
    fc1,
    fc2,
    head,
    normed,
    total,
    theirs,
    parts,
    every,
    tiles,
    load_sem,
    send_sem,
    recv_sem,
    back_send,
    back_recv,
    teach_send,
    teach_recv,
    side_send,
    side_recv,
    right_send,
    right_recv,
    left_send,
    left_recv,
    twin_send,
    twin_recv,
):
    dp = lax.axis_index("dp")
    me = lax.axis_index("fsdp")
    tokens, width = hidden.shape
    seq, texts = text_ids.shape
    units = fc1.shape[0]
    window = slabs.shape[0]
    phases, _, pairs, rows_here, _ = every.shape
    chunk = tokens // phases
    quarter = chunk // 2
    quarters = 2 * phases
    slots = texts // phases
    loads = [
        pltpu.make_async_copy(src, dst, load_sem.at[i])
        for i, (src, dst) in enumerate(((fc1_hbm, fc1), (fc2_hbm, fc2), (head_hbm, head)))
    ]
    for load in loads:
        load.start()

    column = count // 4
    ring = 2 * column
    core = lax.rem(dp, 2)
    y = lax.rem(dp // 2, 2)
    z = dp // 4
    place = jnp.where(y == 0, z, ring - 1 - z)

    def at_place(p, c):
        p = lax.rem(p + 2 * ring, ring)
        return jnp.where(p < column, 4 * p, 4 * (ring - 1 - p) + 2) + c

    right = at_place(place + 1, core)
    left = at_place(place - 1, core)
    twin = dp + 1 - 2 * core

    def ahead(by):
        return (dp, lax.rem(me + by + n, n))

    def later(s):
        return lax.rem(dp + s + count, count)

    tiles[...] = jnp.zeros_like(tiles)
    barrier = pltpu.get_barrier_semaphore()
    near = [ahead(by) for by in range(1, n)] + [(right, me), (left, me), (twin, me)]
    for other in near:
        pl.semaphore_signal(barrier, inc=1, device_id=other, device_id_type=MESH)

    def greet(s, _):
        pl.semaphore_signal(barrier, inc=1, device_id=(later(-s), me), device_id_type=MESH)
        return 0

    lax.fori_loop(1, window, greet, 0)

    def copy(src, dst, send, recv, to):
        return pltpu.make_async_remote_copy(
            src_ref=src, dst_ref=dst, send_sem=send, recv_sem=recv, device_id=to, device_id_type=MESH
        )

    def outward(by, c):
        rows = pl.ds(c * quarter, quarter)
        return copy(
            normed.at[rows],
            theirs.at[by - 1, rows],
            send_sem.at[by - 1, c],
            recv_sem.at[by - 1, c],
            ahead(by),
        )

    def homeward(by, c):
        rows = pl.ds(c * quarter, quarter)
        return copy(
            theirs.at[by - 1, rows],
            parts.at[by - 1, rows],
            back_send.at[by - 1, c],
            back_recv.at[by - 1, c],
            ahead(-by),
        )

    def lesson(s, block):
        return copy(slabs.at[s], tiles.at[lax.rem(block, 2), block // 2], teach_send.at[s], teach_recv.at[s], (later(s), me))

    def normalise(c):
        rows = pl.ds(c * chunk, chunk)
        normed[rows, :] = layer_norm(
            hidden[rows, :].astype(F32), ln_gain[...], ln_bias[...]
        ).astype(BF16)

    def go_out(c):
        for by in range(1, n):
            outward(by, c).start()

    def go_home(c):
        for by in range(1, n):
            homeward(by, c).start()

    normalise(0)
    pl.semaphore_wait(barrier, n + 2 + window - 1)
    go_out(0)
    go_out(1)

    def teach(s, _):
        turned = teacher[s].astype(F32).T
        for f in range(n):
            for h in range(phases):
                low = (f * phases + h) * slots
                slabs[s, h, f * slots : (f + 1) * slots, :] = turned[low : low + slots].astype(
                    BF16
                )

        @pl.when(s > 0)
        def _():
            lesson(s, dp).start()

        return 0

    lax.fori_loop(0, window, teach, 0)
    tiles[core, dp // 2] = slabs[0]
    for c in range(1, phases):
        normalise(c)
    for f in range(n):

        @pl.when(me == f)
        def _():
            bias[...] = fc1_bias[f * units : (f + 1) * units].reshape(1, units)

    kept_rows[...] = (text_ids[...] != 0).astype(F32).T
    picture = unit_rows(images[...].astype(F32)).astype(BF16)
    loads[0].wait()
    loads[1].wait()

    def mlp(values):
        mixed = None
        for low in range(0, units, tile):
            high = min(low + tile, units)
            pre = lax.dot_general(
                values, fc1[low:high, :], (((1,), (1,)), ((), ())), preferred_element_type=F32
            )
            act = jax.nn.gelu(pre + bias[:, low:high], approximate=True).astype(BF16)
            term = jnp.dot(act, fc2[low:high, :], preferred_element_type=F32)
            mixed = term if mixed is None else mixed + term
        return mixed

    def own(c):
        rows = pl.ds(c * chunk, chunk)
        total[rows, :] = mlp(normed[rows, :]) + hidden[rows, :].astype(F32) + fc2_bias[...]

    def their(c):
        rows = pl.ds(pl.multiple_of(c * quarter, quarter), quarter)
        for by in range(1, n):
            outward(by, c).wait_recv()

        def one(slot, _):
            theirs[slot, rows, :] = mlp(theirs[slot, rows, :]).astype(BF16)
            return 0

        lax.fori_loop(0, n - 1, one, 0)

    def early(c, _):
        their(c)
        go_home(c)
        go_out(c + 2)
        return 0

    own(0)
    lax.fori_loop(0, 2, early, 0)
    own(1)
    their(2)
    go_home(2)
    loads[2].wait()

    def embed(c):
        rows = pl.ds(c * chunk, chunk)
        out = total[rows, :]
        for by in range(1, n):
            homeward(by, 2 * c).wait_recv()
            homeward(by, 2 * c + 1).wait_recv()
            out = out + parts[by - 1, rows, :].astype(F32)
        final = layer_norm(out, final_gain[...], final_bias[...])
        kept = kept_rows[pl.ds(c * slots, slots), :]
        summed = jnp.sum(final.reshape(slots, seq, width) * kept[:, :, None], axis=1)
        pooled = summed / jnp.sum(kept, axis=1, keepdims=True)
        emb = (
            jnp.dot(pooled.astype(BF16), head[...], preferred_element_type=F32) + head_bias[...]
        )
        return unit_rows(emb).astype(BF16)

    sent = []

    def begin(block, send, recv, to):
        out = copy(block, block, send, recv, to)
        out.start()
        sent.append(out)

    def part(h, f):
        return every.at[h, core, dp // 2, pl.ds(pl.multiple_of(f * slots, slots), slots)]

    def exchange(h):
        every[h, core, dp // 2, pl.ds(pl.multiple_of(me * slots, slots), slots), :] = embed(h)
        for by in range(1, n):
            begin(part(h, me), side_send.at[h, by - 1], side_recv.at[h, by - 1], ahead(by))

    to_right = ring // 2
    to_left = ring - 1 - to_right

    def side_in(h):
        for by in range(1, n):
            block = part(h, lax.rem(me - by + n, n))
            copy(block, block, side_send.at[h, by - 1], side_recv.at[h, by - 1], ahead(by)).wait_recv()

    def set_off(h):
        block = every.at[h, core, dp // 2]
        begin(block, right_send.at[h, 0], right_recv.at[h, 0], (right, me))
        if to_left > 0:
            begin(block, left_send.at[h, 0], left_recv.at[h, 0], (left, me))
        begin(block, twin_send.at[h, 0], twin_recv.at[h, 0], (twin, me))

    def circulate(h):
        twins = 1
        for step in range(1, to_right + 1):
            block = every.at[h, core, at_place(place - step, 0) // 2]
            copy(
                block, block, right_send.at[h, step - 1], right_recv.at[h, step - 1], (right, me)
            ).wait_recv()
            if step < to_right:
                begin(block, right_send.at[h, step], right_recv.at[h, step], (right, me))
            begin(block, twin_send.at[h, twins], twin_recv.at[h, twins], (twin, me))
            twins += 1
            if step <= to_left:
                block = every.at[h, core, at_place(place + step, 0) // 2]
                copy(
                    block, block, left_send.at[h, step - 1], left_recv.at[h, step - 1], (left, me)
                ).wait_recv()
                if step < to_left:
                    begin(block, left_send.at[h, step], left_recv.at[h, step], (left, me))
                begin(block, twin_send.at[h, twins], twin_recv.at[h, twins], (twin, me))
                twins += 1

    def twins_in(h):
        twins = 0
        for step in range(to_right + 1):
            sources = [place - step]
            if 0 < step <= to_left:
                sources.append(place + step)
            for source in sources:
                block = every.at[h, 1 - core, at_place(source, 0) // 2]
                copy(
                    block, block, twin_send.at[h, twins], twin_recv.at[h, twins], (twin, me)
                ).wait_recv()
                twins += 1

    scale = scale_ref[0]
    offset = offset_ref[0]
    pictures = images.shape[0]
    span = (pairs, rows_here, pictures)
    pair = lax.broadcasted_iota(jnp.int32, span, 0)

    def gradient(h, side):
        group = every[h, side].reshape(pairs * rows_here, width)
        dots = lax.dot_general(
            group, picture, (((1,), (1,)), ((), ())), preferred_element_type=F32
        )
        score = (scale * dots + offset).reshape(span)
        gap = jax.nn.sigmoid(score) - jax.nn.sigmoid(tiles[side, :, h].astype(F32))
        behind = dp - side - 2 * pair
        met = jnp.where(behind < 0, behind + count, behind) < window
        weight = jnp.where(met, gap, 0.0).astype(BF16).reshape(pairs * rows_here, pictures)
        return lax.dot_general(
            weight, group, (((0,), (0,)), ((), ())), preferred_element_type=F32
        )

    def taught(s, _):
        lesson(s, later(-s)).wait_recv()
        return 0

    exchange(0)
    side_in(0)
    set_off(0)
    their(3)
    go_home(3)
    circulate(0)
    twins_in(0)
    lax.fori_loop(1, window, taught, 0)
    exchange(1)
    grad[...] = gradient(0, core) + gradient(0, 1 - core)
    side_in(1)
    set_off(1)
    circulate(1)
    grad[...] += gradient(1, core)
    twins_in(1)
    grad[...] += gradient(1, 1 - core)

    def told(s, _):
        lesson(s, dp).wait_send()
        return 0

    lax.fori_loop(1, window, told, 0)
    for by in range(1, n):
        for c in range(quarters):
            outward(by, c).wait_send()
            homeward(by, c).wait_send()
    for out in sent:
        out.wait_send()


def on_device(
    hidden,
    text_ids,
    ln_gain,
    ln_bias,
    fc1_weight,
    fc1_bias,
    fc2_weight,
    fc2_bias,
    final_gain,
    final_bias,
    head_weight,
    head_bias,
    image_emb,
    teacher_logits,
    logit_scale,
    logit_bias,
):
    tokens, width = hidden.shape
    texts = text_ids.shape[0]
    units = fc1_weight.shape[1]
    group, window, pictures = teacher_logits.shape
    n = lax.axis_size("fsdp")
    count = lax.axis_size("dp")
    phases = 2
    slots = texts // phases
    others = max(n - 1, 1)

    vmem = pl.BlockSpec(memory_space=pltpu.VMEM)
    smem = pl.BlockSpec(memory_space=pltpu.SMEM)
    hbm = pl.BlockSpec(memory_space=pl.ANY)
    dma = pltpu.SemaphoreType.DMA
    ring = count // 2
    total = pl.pallas_call(
        functools.partial(tower_kernel, n, count, 768),
        out_shape=jax.ShapeDtypeStruct((pictures, width), F32),
        in_specs=[vmem] * 4 + [hbm, vmem, hbm, vmem, vmem, vmem, hbm, vmem, vmem, vmem, smem, smem],
        out_specs=vmem,
        scratch_shapes=[
            pltpu.VMEM((window, phases, n * slots, pictures), BF16),
            pltpu.VMEM((1, units), F32),
            pltpu.VMEM((texts, text_ids.shape[1]), F32),
            pltpu.VMEM((units, width), BF16),
            pltpu.VMEM(fc2_weight.shape, BF16),
            pltpu.VMEM(head_weight.shape, BF16),
            pltpu.VMEM((tokens, width), BF16),
            pltpu.VMEM((tokens, width), F32),
            pltpu.VMEM((others, tokens, width), BF16),
            pltpu.VMEM((others, tokens, width), BF16),
            pltpu.VMEM((phases, 2, count // 2, n * slots, width), BF16),
            pltpu.VMEM((2, count // 2, phases, n * slots, pictures), BF16),
            dma((3,)),
            dma((others, 2 * phases)),
            dma((others, 2 * phases)),
            dma((others, 2 * phases)),
            dma((others, 2 * phases)),
            dma((window,)),
            dma((window,)),
            dma((phases, others)),
            dma((phases, others)),
        ]
        + [dma((phases, ring))] * 6,
        compiler_params=pltpu.CompilerParams(
            collective_id=0, has_side_effects=True, vmem_limit_bytes=62 * 1024 * 1024
        ),
        cost_estimate=pl.CostEstimate(
            flops=4 * n * tokens * width * units,
            bytes_accessed=4 * width * units,
            transcendentals=n * tokens * units,
        ),
    )(
        hidden,
        text_ids.T,
        ln_gain,
        ln_bias,
        fc1_weight.T,
        fc1_bias,
        fc2_weight,
        fc2_bias,
        final_gain,
        final_bias,
        head_weight,
        head_bias,
        image_emb,
        jnp.transpose(teacher_logits, (1, 2, 0)),
        logit_scale,
        logit_bias,
    )
    return logit_scale[0] * total


def solution(mesh):
    placed = (
        P(("dp", "fsdp"), None),
        P(("dp", "fsdp"), None),
        P(),
        P(),
        P(None, "fsdp"),
        P(),
        P("fsdp", None),
        P(),
        P(),
        P(),
        P(),
        P(),
        P(("dp", "fsdp"), None),
        P("dp", None, "fsdp"),
        P(),
        P(),
    )
    return jax.shard_map(
        on_device, mesh=mesh, in_specs=placed, out_specs=P(("dp", "fsdp"), None), check_vma=False
    )
```
